32 devices in a mesh: ang: 8 (over z, x), rad: 4 (over y, core).
Axes of the slice: x: 2, y: 2, z: 4, core: 2. Of those that a mesh axis runs over, the one named last changes fastest.
Arguments:
- right_side: float32 [64, 512, 256], P('rad', 'ang'), may hold values from -6 to 6
- conduct: float32 [64, 512], P('rad', 'ang'), may hold values from 0.25 to 4
- local_inverse: bfloat16 [8, 4, 1024, 1024], P('ang', 'rad'), may hold values from -1 to 3, as said below
- primal_basis: float32 [8, 4, 1024, 16], P('ang', 'rad'), may hold values from -0.22297633 to 0.22297633
- coarse_inverse: float32 [16, 16], replicated, may hold values from -1 to 3, as said below
Outputs:
- solution_field: float32 [64, 512, 256], P('rad', 'ang')
The draws below stay inside these ranges and needn't reach their ends.
Inputs may be any that keep to these rules, and one draw needn't show every extreme that they name: `local_inverse`: each block is symmetric positive definite. `coarse_inverse`: symmetric positive definite.
All inputs are finite; a program needn't handle non-finite values.
Results may differ from the reference program's by a relative error of at most 0.0027.
Values sent between devices are 32-bit elements; how exact they have to be, the bound alone decides.
A program may use at most 64 MiB of HBM per device.

```python
import math
import jax
import jax.numpy as jnp
from jax import lax

LR = 16
LA = 64
COLS = 256
KPRIM = 16
ITERS = 3
NCELL = 1024
SA = 8
SR = 4
NR = 64
NA = 512


def definite_blocks(key, lead, order):
    first, second = jax.random.split(key)
    spread = 0.9 / math.sqrt(order)
    offdiag = jax.random.uniform(first, lead + (order, order), jnp.float32, -spread, spread)
    offdiag = 0.5 * (offdiag + jnp.swapaxes(offdiag, -1, -2))
    diagonal = jax.random.uniform(second, lead + (order,), jnp.float32, 1.0, 2.5)
    identity = jnp.eye(order, dtype=jnp.float32)
    return offdiag * (1.0 - identity) + diagonal[..., None] * identity


def draw_local_inverse(key, part):
    return definite_blocks(jax.random.fold_in(key, 11), (SA, SR), NCELL).astype(jnp.bfloat16)


def draw_coarse_inverse(key, part):
    return definite_blocks(jax.random.fold_in(key, 23), (), KPRIM)


def block_levels(stream_key, dims, shards, smallest, largest):
    loudness = 1.0
    for position, shards_of in shards:
        steps = jax.random.uniform(jax.random.fold_in(jax.random.fold_in(stream_key, 6), position), (shards_of,), jnp.float32, smallest / len(shards), largest / len(shards))
        loudness = loudness * jnp.repeat(jnp.exp(steps), dims[position] // shards_of).reshape((-1,) + (1,) * (len(dims) - 1 - position))
    return loudness


def bell_draw(stream_key, shape, deviation, reach, cuts=(), held_as=jnp.bfloat16):
    gain = block_levels(stream_key, shape, cuts, -0.22, 0.18) if cuts else 1.0
    entries = jax.random.normal(stream_key, shape, jnp.float32) * deviation * gain
    return jnp.minimum(jnp.maximum(entries, -reach), reach).astype(held_as)


def setup_inputs(seed: int = 0) -> dict:
    key_list = jax.random.split(jax.random.key(seed), 6)
    return {
        "right_side": bell_draw(key_list[0], (NR, NA, COLS), 1.0, 6.0, ((0, 4), (1, 8)), jnp.float32),
        "conduct": jnp.clip(jnp.exp(math.log(4.0) - 2.7725887 * jax.random.uniform(key_list[1], (NR, NA), jnp.float32) ** block_levels(key_list[1], (NR, NA), ((0, 4), (1, 8)), -0.2, 0.2)), 0.25, 4.0),
        "local_inverse": draw_local_inverse(jax.random.fold_in(key_list[5], 71), 0),
        "primal_basis": bell_draw(key_list[3], (SA, SR, NCELL, KPRIM), ((NCELL * SA * SR * KPRIM) ** -0.25), 0.22297633, ((0, 8), (1, 4)), jnp.float32),
        "coarse_inverse": draw_coarse_inverse(jax.random.fold_in(key_list[5], 71), 0),
    }


def operate(field, conduct):
    padded = jnp.pad(field, ((1, 1), (0, 0), (0, 0)))
    radial = padded[2:] + padded[:-2]
    angular = jnp.roll(field, 1, axis=1) + jnp.roll(field, -1, axis=1)
    return (4.0 + conduct)[:, :, None] * field - radial - angular


def to_blocks(field):
    cols = field.shape[2]
    shaped = field.reshape(SR, LR, SA, LA, cols).transpose(2, 0, 1, 3, 4)
    return shaped.reshape(SA, SR, NCELL, cols)


def from_blocks(blocks):
    cols = blocks.shape[3]
    shaped = blocks.reshape(SA, SR, LR, LA, cols).transpose(1, 2, 0, 3, 4)
    return shaped.reshape(NR, NA, cols)


def precondition(residual, local_inverse, primal_basis, coarse_inverse):
    blocks = to_blocks(residual)
    coarse = jnp.einsum("abnk,abnc->kc", primal_basis, blocks, precision=lax.Precision.HIGHEST)
    coarse_z = jnp.dot(coarse_inverse, coarse, precision=lax.Precision.HIGHEST)

    def one_cycle(packed):
        inverse_row, basis_row, block_row = packed
        rounded = lax.optimization_barrier(block_row.astype(jnp.bfloat16))
        local = jnp.einsum("bnm,bmc->bnc", inverse_row.astype(jnp.float32), rounded.astype(jnp.float32))
        lifted = jnp.einsum("bnk,kc->bnc", basis_row, coarse_z, precision=lax.Precision.HIGHEST)
        return local + lifted

    zed = lax.map(one_cycle, (local_inverse, primal_basis, blocks))
    return from_blocks(zed)


def reference(right_side, conduct, local_inverse, primal_basis, coarse_inverse):
    solution_field = jnp.zeros_like(right_side)
    residual = right_side
    zed = precondition(residual, local_inverse, primal_basis, coarse_inverse)
    product = jnp.sum(residual * zed, axis=(0, 1))
    direction = zed
    for step in range(ITERS):
        image = operate(direction, conduct)
        alpha = product / jnp.sum(direction * image, axis=(0, 1))
        solution_field = solution_field + alpha * direction
        residual = residual - alpha * image
        if step + 1 < ITERS:
            zed = precondition(residual, local_inverse, primal_basis, coarse_inverse)
            fresh = jnp.sum(residual * zed, axis=(0, 1))
            direction = zed + (fresh / product) * direction
            product = fresh
    return solution_field
```

```python
import functools
import jax
import jax.numpy as jnp
from jax import lax
from jax.experimental import pallas as pl
from jax.experimental.pallas import tpu as pltpu
from jax.sharding import PartitionSpec as P

ITERS = 3
F32 = jnp.float32
BF16 = jnp.bfloat16
MESH = pl.DeviceIdType.MESH


def stage_radices(n_ang):
    first = 2 if n_ang % 2 == 0 else 1
    radices, rest = [], n_ang // first
    while rest > 1:
        factor = 4 if rest % 4 == 0 else next(f for f in range(2, rest + 1) if rest % f == 0)
        radices.append(factor)
        rest //= factor
    return first, radices


def split(value):
    high = value.astype(BF16)
    return high, (value - high.astype(F32)).astype(BF16)


def kernel(dims, rhs_hbm, cond_hbm, inv_hbm, basis_hbm, coarse_hbm, out_ref,
           lx, rhs, right, image, zed, direction, diag, cond, coarse_inv,
           basis, lift, ybufs, edges, pack, *rest):
    n_ang, n_rad, lr, la, cols, kprim, first, radices = dims
    nst = 1 + len(radices)
    recvs = rest[:nst]
    (load_sem, basis_send, basis_recv, edge_send, edge_recv) = rest[nst:nst + 5]
    ar_sems = rest[nst + 5:]
    ncell = lr * la
    main, bottom = la, la + ncell
    left, rightside = bottom + la, bottom + la + lr
    total = rightside + lr

    ang, rad = lax.axis_index("ang"), lax.axis_index("rad")
    ang_up, ang_down = lax.rem(ang + 1, n_ang), lax.rem(ang + n_ang - 1, n_ang)

    loads = [
        pltpu.make_async_copy(basis_hbm, basis.at[pl.ds(main, ncell)], load_sem.at[0]),
        pltpu.make_async_copy(rhs_hbm, rhs, load_sem.at[1]),
        pltpu.make_async_copy(inv_hbm, lx.at[pl.ds(0, ncell)], load_sem.at[2]),
        pltpu.make_async_copy(cond_hbm, cond, load_sem.at[3]),
        pltpu.make_async_copy(coarse_hbm, coarse_inv, load_sem.at[4]),
    ]
    for load in loads:
        load.start()

    def partners(stage):
        found = []
        if stage == 0:
            size = n_rad * first
            low = lax.rem(ang, first)
            rank = rad * first + low
            for o in range(1, size):
                other = lax.rem(rank + o, size)
                found.append((ang - low + lax.rem(other, first), other // first))
        else:
            stride = first
            for f in radices[:stage - 1]:
                stride *= f
            f = radices[stage - 1]
            digit = lax.rem(ang // stride, f)
            for o in range(1, f):
                other = lax.rem(digit + o, f)
                found.append((ang + (other - digit) * stride, rad))
        return found

    basis[pl.ds(0, la)] = jnp.zeros((la, kprim), F32)
    basis[pl.ds(bottom, la)] = jnp.zeros((la, kprim), F32)
    for k in range(ITERS):
        ybufs[k, pl.ds(0, la)] = jnp.zeros((la, cols), F32)
        ybufs[k, pl.ds(bottom, la)] = jnp.zeros((la, cols), F32)

    groups = [partners(s) for s in range(nst)]
    barrier = pltpu.get_barrier_semaphore()
    greeted = [p for g in groups for p in g] + [(ang_up, rad), (ang_down, rad)]
    for peer in greeted:
        pl.semaphore_signal(barrier, inc=1, device_id=peer, device_id_type=MESH)

    def gather_edges(src, dst):
        for r in range(lr):
            dst[0, pl.ds(r, 1)] = src[pl.ds(main + r * la, 1)]
            dst[1, pl.ds(r, 1)] = src[pl.ds(main + r * la + la - 1, 1)]

    def exchange(buf, edge, send, recv):
        def remote(src, dst, i, peer):
            return pltpu.make_async_remote_copy(
                src_ref=src, dst_ref=dst, send_sem=send.at[i], recv_sem=recv.at[i],
                device_id=peer, device_id_type=MESH)
        upward = remote(buf.at[pl.ds(bottom - la, la)], buf.at[pl.ds(0, la)], 0, (ang, rad + 1))
        downward = remote(buf.at[pl.ds(main, la)], buf.at[pl.ds(bottom, la)], 1, (ang, rad - 1))
        ahead = remote(edge.at[1], buf.at[pl.ds(left, lr)], 2, (ang_up, rad))
        behind = remote(edge.at[0], buf.at[pl.ds(rightside, lr)], 3, (ang_down, rad))
        return upward, downward, ahead, behind

    def start_exchange(copies):
        upward, downward, ahead, behind = copies
        pl.when(rad < n_rad - 1)(upward.start)
        pl.when(rad > 0)(downward.start)
        ahead.start()
        behind.start()

    def finish_exchange(copies):
        upward, downward, ahead, behind = copies
        pl.when(rad > 0)(upward.wait_recv)
        pl.when(rad < n_rad - 1)(downward.wait_recv)
        ahead.wait_recv()
        behind.wait_recv()
        pl.when(rad < n_rad - 1)(upward.wait_send)
        pl.when(rad > 0)(downward.wait_send)
        ahead.wait_send()
        behind.wait_send()

    def reduce(phase, rows, value):
        pack[phase, 0, pl.ds(0, rows)] = value
        for stage in range(nst):
            send, recv = ar_sems[2 * stage], ar_sems[2 * stage + 1]
            copies = []
            for o, peer in enumerate(groups[stage]):
                copies.append(pltpu.make_async_remote_copy(
                    src_ref=pack.at[phase, stage, pl.ds(0, rows)],
                    dst_ref=recvs[stage].at[phase, o, pl.ds(0, rows)],
                    send_sem=send.at[phase, o], recv_sem=recv.at[phase, o],
                    device_id=peer, device_id_type=MESH))
            for copy in copies:
                copy.start()
            acc = value
            for o, copy in enumerate(copies):
                copy.wait_recv()
                acc = acc + recvs[stage][phase, o, pl.ds(0, rows)]
            value = acc
            if stage + 1 < nst:
                pack[phase, stage + 1, pl.ds(0, rows)] = value
            pending.extend(copies)
        return value

    pending = []

    loads[0].wait()
    gather_edges(basis, basis_edge := rest[-1])
    pl.semaphore_wait(barrier, len(greeted))
    basis_copies = exchange(basis, basis_edge, basis_send, basis_recv)
    start_exchange(basis_copies)

    row16 = lax.broadcasted_iota(jnp.int32, (kprim, 3 * kprim), 0)
    col48 = lax.broadcasted_iota(jnp.int32, (kprim, 3 * kprim), 1)
    pick_high = jnp.logical_or(col48 == row16, col48 == row16 + 2 * kprim).astype(F32).astype(BF16)
    pick_low = (col48 == row16 + kprim).astype(F32).astype(BF16)

    def make_lift(start, size):
        high, low = split(basis[pl.ds(start, size)])
        both = (jnp.dot(high, pick_high, preferred_element_type=F32)
                + jnp.dot(low, pick_low, preferred_element_type=F32))
        lift[pl.ds(start, size)] = both.astype(BF16)

    make_lift(main, ncell)
    row32 = lax.broadcasted_iota(jnp.int32, (2 * kprim, 3 * kprim), 0)
    col32 = lax.broadcasted_iota(jnp.int32, (2 * kprim, 3 * kprim), 1)
    flip = (row32 == col32).astype(F32).astype(BF16)
    lx[pl.ds(ncell, 2 * kprim)] = lax.dot_general(
        flip, lift[pl.ds(main, ncell)], (((1,), (1,)), ((), ())),
        preferred_element_type=F32).astype(BF16)

    loads[3].wait()
    loads[4].wait()
    eye = (lax.broadcasted_iota(jnp.int32, (la, la), 0) == lax.broadcasted_iota(jnp.int32, (la, la), 1))
    for r in range(lr):
        column = jnp.sum(jnp.where(eye, cond[pl.ds(r, 1)], 0.0), axis=1, keepdims=True)
        diag[pl.ds(r * la, la)] = jnp.broadcast_to(4.0 + column, (la, 128))

    def store_split(start, value):
        high, low = split(value)
        right[pl.ds(start, la), pl.ds(0, cols)] = high
        right[pl.ds(start, la), pl.ds(cols, cols)] = low

    tile = 256 if ncell % 256 == 0 else la

    def apply_local(vec, out):
        def body(i, acc):
            start = pl.multiple_of(i * tile, tile)
            prod = jnp.dot(lx[pl.ds(start, tile)], right[...], preferred_element_type=F32)
            got = prod[:, :cols] + prod[:, cols:]
            out[pl.ds(main + start, tile)] = got
            part = got * vec[pl.ds(start, tile)]
            return acc + jnp.sum(part.reshape(tile // 8, 8, cols), axis=0)
        acc = lax.fori_loop(0, ncell // tile, body, jnp.zeros((8, cols), F32))
        small = jnp.dot(lx[pl.ds(ncell, 2 * kprim)], right[...], preferred_element_type=F32)
        both = small[:, :cols] + small[:, cols:]
        return jnp.sum(acc, axis=0, keepdims=True), both[:kprim] + both[kprim:]

    def lifted_weights(coarse):
        weights = jnp.dot(coarse_inv[...], coarse, precision=lax.Precision.HIGHEST, preferred_element_type=F32)
        high, low = split(weights)
        energy = jnp.sum(coarse * weights, axis=0, keepdims=True)
        return jnp.concatenate([high, high, low], axis=0), energy

    step_rows = 2 * lr if total % (2 * lr) == 0 else 16
    loads[1].wait()

    def split_rhs(r, carry):
        start = pl.multiple_of(r * la, la)
        store_split(start, rhs[pl.ds(start, la)])
        return carry
    lax.fori_loop(0, lr, split_rhs, 0)
    loads[2].wait()

    rows_in = lax.broadcasted_iota(jnp.int32, (la, cols), 0)

    def apply_operator():
        def body(r, acc):
            at = pl.multiple_of(r * la, la)
            here = direction[pl.ds(at + la, la)]
            radial = direction[pl.ds(at, la)] + direction[pl.ds(at + 2 * la, la)]
            before = jnp.where(rows_in == 0, direction[pl.ds(left + r, 1)], pltpu.roll(here, 1, 0))
            after = jnp.where(rows_in == la - 1, direction[pl.ds(rightside + r, 1)], pltpu.roll(here, la - 1, 0))
            weight = diag[pl.ds(at, la)]
            weight = jnp.concatenate([weight] * (cols // 128), axis=1)
            got = weight * here - ((before + after) + radial)
            image[pl.ds(at, la)] = got
            store_split(at, got)
            return acc + jnp.sum((got * here).reshape(la // 8, 8, cols), axis=0)
        acc = lax.fori_loop(0, lr, body, jnp.zeros((8, cols), F32))
        return jnp.sum(acc, axis=0, keepdims=True)

    product = None
    alpha = None
    for k in range(ITERS):
        ybuf = ybufs.at[k]
        if k == 0:
            inner, coarse = apply_local(rhs, ybuf)
            curve = jnp.zeros((1, cols), F32)
        else:
            inner, coarse = apply_local(image, ybuf)
        edge = edges.at[k]
        gather_edges(ybuf, edge)
        copies = exchange(ybuf, edge, edge_send.at[k], edge_recv.at[k])
        start_exchange(copies)
        value = jnp.concatenate(
            [coarse, inner, curve, jnp.zeros((6, cols), F32)], axis=0)
        value = reduce(k, kprim + 8, value)
        coarse, inner, curve = value[:kprim], value[kprim:kprim + 1], value[kprim + 1:kprim + 2]
        weights, energy = lifted_weights(coarse)
        inner = inner + energy
        if k == 0:
            finish_exchange(basis_copies)
            make_lift(0, la)
            make_lift(bottom, total - bottom)
        finish_exchange(copies)
        if k == 0:
            product = inner

            def begin(i, carry):
                at = pl.multiple_of(i * step_rows, step_rows)
                got = ybuf[pl.ds(at, step_rows)] + jnp.dot(
                    lift[pl.ds(at, step_rows)], weights, preferred_element_type=F32)
                zed[pl.ds(at, step_rows)] = got
                direction[pl.ds(at, step_rows)] = got
                return carry
            lax.fori_loop(0, total // step_rows, begin, 0)
        else:
            alpha = product / curve
            fresh = alpha * alpha * inner - product
            ratio = fresh / product
            product = fresh

            def update(i, carry):
                at = pl.multiple_of(i * step_rows, step_rows)
                got = ybuf[pl.ds(at, step_rows)] + jnp.dot(
                    lift[pl.ds(at, step_rows)], weights, preferred_element_type=F32)
                fresh_zed = zed[pl.ds(at, step_rows)] - alpha * got
                zed[pl.ds(at, step_rows)] = fresh_zed
                old = direction[pl.ds(at, step_rows)]
                moved = alpha * old
                if k > 1:
                    moved = moved + solution_acc[pl.ds(at, step_rows)]
                solution_acc[pl.ds(at, step_rows)] = moved
                direction[pl.ds(at, step_rows)] = fresh_zed + ratio * old
                return carry
            solution_acc = rest[-2]
            lax.fori_loop(0, total // step_rows, update, 0)
        curve = apply_operator()
    curve = reduce(ITERS, 8, jnp.broadcast_to(curve, (8, cols)))[:1]
    alpha = product / curve

    def finish(r, carry):
        at = pl.multiple_of(r * la, la)
        out_ref[pl.ds(at, la)] = solution_acc[pl.ds(at + la, la)] + alpha * direction[pl.ds(at + la, la)]
        return carry
    lax.fori_loop(0, lr, finish, 0)
    for copy in pending:
        copy.wait_send()


def per_device(n_ang, n_rad, right_side, conduct, local_inverse, primal_basis, coarse_inverse):
    lr, la, cols = right_side.shape
    ncell, kprim = primal_basis.shape[2:]
    first, radices = stage_radices(n_ang)
    sizes = [n_rad * first] + radices
    nst = len(sizes)
    total = ncell + 2 * la + 2 * lr
    rows = kprim + 8
    dma = pltpu.SemaphoreType.DMA
    scratch = [
        pltpu.VMEM((ncell + 2 * kprim, ncell), BF16),
        pltpu.VMEM((ncell, cols), F32),
        pltpu.VMEM((ncell, 2 * cols), BF16),
        pltpu.VMEM((ncell, cols), F32),
        pltpu.VMEM((total, cols), F32),
        pltpu.VMEM((total, cols), F32),
        pltpu.VMEM((ncell, 128), F32),
        pltpu.VMEM((lr, la), F32),
        pltpu.VMEM((kprim, kprim), F32),
        pltpu.VMEM((total, kprim), F32),
        pltpu.VMEM((total, 3 * kprim), BF16),
        pltpu.VMEM((ITERS, total, cols), F32),
        pltpu.VMEM((ITERS, 2, lr, cols), F32),
        pltpu.VMEM((ITERS + 1, nst, rows, cols), F32),
    ]
    scratch += [pltpu.VMEM((ITERS + 1, s - 1, rows, cols), F32) for s in sizes]
    scratch += [dma((5,)), dma((4,)), dma((4,)), dma((ITERS, 4)), dma((ITERS, 4))]
    for s in sizes:
        scratch += [dma((ITERS + 1, s - 1)), dma((ITERS + 1, s - 1))]
    scratch += [pltpu.VMEM((total, cols), F32), pltpu.VMEM((2, lr, kprim), F32)]
    flat = pl.pallas_call(
        functools.partial(kernel, (n_ang, n_rad, lr, la, cols, kprim, first, radices)),
        out_shape=jax.ShapeDtypeStruct((ncell, cols), F32),
        in_specs=[pl.BlockSpec(memory_space=pl.ANY)] * 5,
        out_specs=pl.BlockSpec(memory_space=pltpu.VMEM),
        scratch_shapes=scratch,
        compiler_params=pltpu.CompilerParams(
            collective_id=0, has_side_effects=True, vmem_limit_bytes=48 * 1024 * 1024),
        cost_estimate=pl.CostEstimate(
            flops=2 * ITERS * ncell * ncell * 2 * cols, bytes_accessed=5 * 1024 * 1024, transcendentals=0),
    )(right_side.reshape(ncell, cols), conduct, local_inverse.reshape(ncell, ncell),
      primal_basis.reshape(ncell, kprim), coarse_inverse)
    return flat.reshape(lr, la, cols)


def solution(mesh):
    return jax.shard_map(
        functools.partial(per_device, mesh.shape["ang"], mesh.shape["rad"]),
        mesh=mesh,
        in_specs=(
            P("rad", "ang", None),
            P("rad", "ang"),
            P("ang", "rad", None, None),
            P("ang", "rad", None, None),
            P(),
        ),
        out_specs=P("rad", "ang", None),
        check_vma=False,
    )
```

```python
import functools
import jax
import jax.numpy as jnp
from jax import lax
from jax.experimental import pallas as pl
from jax.experimental.pallas import tpu as pltpu
from jax.sharding import PartitionSpec as P

ITERS = 3
F32 = jnp.float32
BF16 = jnp.bfloat16
MESH = pl.DeviceIdType.MESH


def stage_radices(n_ang):
    first = 2 if n_ang % 2 == 0 else 1
    radices, rest = [], n_ang // first
    while rest > 1:
        factor = 4 if rest % 4 == 0 else next(f for f in range(2, rest + 1) if rest % f == 0)
        radices.append(factor)
        rest //= factor
    return first, radices


def split(value):
    high = value.astype(BF16)
    return high, (value - high.astype(F32)).astype(BF16)


def kernel(dims, rhs_hbm, cond_hbm, inv_hbm, basis_hbm, coarse_hbm, out_ref,
           lx, rhs, right, image, zed, direction, diag, cond, coarse_inv,
           basis_t, basis, lift, ybufs, edges, pack, *rest):
    n_ang, n_rad, lr, la, cols, kprim, first, radices = dims
    nst = 1 + len(radices)
    recvs = rest[:nst]
    (load_sem, basis_send, basis_recv, edge_send, edge_recv) = rest[nst:nst + 5]
    ar_sems = rest[nst + 5:]
    ncell = lr * la
    main, bottom = la, la + ncell
    left, rightside = bottom + la, bottom + la + lr
    total = zed.shape[0]
    step_rows = total // (total // 256)

    ang, rad = lax.axis_index("ang"), lax.axis_index("rad")
    ang_up, ang_down = lax.rem(ang + 1, n_ang), lax.rem(ang + n_ang - 1, n_ang)

    loads = [
        pltpu.make_async_copy(basis_hbm, basis_t, load_sem.at[0]),
        pltpu.make_async_copy(rhs_hbm, rhs, load_sem.at[1]),
        pltpu.make_async_copy(inv_hbm, lx.at[pl.ds(0, ncell)], load_sem.at[2]),
        pltpu.make_async_copy(cond_hbm, cond, load_sem.at[3]),
        pltpu.make_async_copy(coarse_hbm, coarse_inv, load_sem.at[4]),
    ]
    for load in loads:
        load.start()

    def partners(stage):
        found = []
        if stage == 0:
            size = n_rad * first
            low = lax.rem(ang, first)
            rank = rad * first + low
            for o in range(1, size):
                other = lax.rem(rank + o, size)
                found.append((ang - low + lax.rem(other, first), other // first))
        else:
            stride = first
            for f in radices[:stage - 1]:
                stride *= f
            f = radices[stage - 1]
            digit = lax.rem(ang // stride, f)
            for o in range(1, f):
                other = lax.rem(digit + o, f)
                found.append((ang + (other - digit) * stride, rad))
        return found

    basis[pl.ds(0, la)] = jnp.zeros((la, 3 * kprim), F32)
    basis[pl.ds(bottom, total - bottom)] = jnp.zeros((total - bottom, 3 * kprim), F32)
    for k in range(ITERS):
        ybufs[k, pl.ds(0, la)] = jnp.zeros((la, cols), F32)
        ybufs[k, pl.ds(bottom, total - bottom)] = jnp.zeros((total - bottom, cols), F32)

    groups = [partners(s) for s in range(nst)]
    barrier = pltpu.get_barrier_semaphore()
    greeted = [p for g in groups for p in g] + [(ang_up, rad), (ang_down, rad)]
    for peer in greeted:
        pl.semaphore_signal(barrier, inc=1, device_id=peer, device_id_type=MESH)

    def gather_edges(src, dst):
        for r in range(lr):
            dst[0, pl.ds(r, 1)] = src[pl.ds(main + r * la, 1)]
            dst[1, pl.ds(r, 1)] = src[pl.ds(main + r * la + la - 1, 1)]

    def exchange(buf, edge, send, recv):
        def remote(src, dst, i, peer):
            return pltpu.make_async_remote_copy(
                src_ref=src, dst_ref=dst, send_sem=send.at[i], recv_sem=recv.at[i],
                device_id=peer, device_id_type=MESH)
        upward = remote(buf.at[pl.ds(bottom - la, la)], buf.at[pl.ds(0, la)], 0, (ang, rad + 1))
        downward = remote(buf.at[pl.ds(main, la)], buf.at[pl.ds(bottom, la)], 1, (ang, rad - 1))
        ahead = remote(edge.at[1], buf.at[pl.ds(left, lr)], 2, (ang_up, rad))
        behind = remote(edge.at[0], buf.at[pl.ds(rightside, lr)], 3, (ang_down, rad))
        return upward, downward, ahead, behind

    def start_exchange(copies):
        upward, downward, ahead, behind = copies
        pl.when(rad < n_rad - 1)(upward.start)
        pl.when(rad > 0)(downward.start)
        ahead.start()
        behind.start()

    def finish_exchange(copies):
        upward, downward, ahead, behind = copies
        pl.when(rad > 0)(upward.wait_recv)
        pl.when(rad < n_rad - 1)(downward.wait_recv)
        ahead.wait_recv()
        behind.wait_recv()
        pl.when(rad < n_rad - 1)(upward.wait_send)
        pl.when(rad > 0)(downward.wait_send)
        ahead.wait_send()
        behind.wait_send()

    def reduce(phase, rows, value, shadow=None):
        pack[phase, 0, pl.ds(0, rows)] = value
        for stage in range(nst):
            send, recv = ar_sems[2 * stage], ar_sems[2 * stage + 1]
            copies = []
            for o, peer in enumerate(groups[stage]):
                copies.append(pltpu.make_async_remote_copy(
                    src_ref=pack.at[phase, stage, pl.ds(0, rows)],
                    dst_ref=recvs[stage].at[phase, o, pl.ds(0, rows)],
                    send_sem=send.at[phase, o], recv_sem=recv.at[phase, o],
                    device_id=peer, device_id_type=MESH))
            for copy in copies:
                copy.start()
            if stage == 0 and shadow is not None:
                shadow()
            acc = value
            for o, copy in enumerate(copies):
                copy.wait_recv()
                acc = acc + recvs[stage][phase, o, pl.ds(0, rows)]
            value = acc
            if stage + 1 < nst:
                pack[phase, stage + 1, pl.ds(0, rows)] = value
            pending.extend(copies)
        return value

    pending = []

    loads[0].wait()
    high, low = split(basis_t[...])
    lx[pl.ds(ncell, 2 * kprim)] = jnp.concatenate([high, low], axis=0)

    def store_split(start, value):
        high, low = split(value)
        right[pl.ds(start, la), pl.ds(0, cols)] = high
        right[pl.ds(start, la), pl.ds(cols, cols)] = low

    tile = 256 if ncell % 256 == 0 else la

    def apply_local(vec, out):
        def body(i, acc):
            start = pl.multiple_of(i * tile, tile)
            prod = jnp.dot(lx[pl.ds(start, tile)], right[...], preferred_element_type=F32)
            got = prod[:, :cols] + prod[:, cols:]
            out[pl.ds(main + start, tile)] = got
            part = got * vec[pl.ds(start, tile)]
            return acc + jnp.sum(part.reshape(tile // 8, 8, cols), axis=0)
        acc = lax.fori_loop(0, ncell // tile, body, jnp.zeros((8, cols), F32))
        small = jnp.dot(lx[pl.ds(ncell, 2 * kprim)], right[...], preferred_element_type=F32)
        both = small[:, :cols] + small[:, cols:]
        return jnp.sum(acc, axis=0, keepdims=True), both[:kprim] + both[kprim:]

    def lifted_weights(coarse):
        weights = jnp.dot(coarse_inv[...], coarse, precision=lax.Precision.HIGHEST, preferred_element_type=F32)
        high, low = split(weights)
        energy = jnp.sum(coarse * weights, axis=0, keepdims=True)
        return jnp.concatenate([high, high, low], axis=0), energy

    loads[1].wait()

    def split_rhs(r, carry):
        start = pl.multiple_of(r * la, la)
        store_split(start, rhs[pl.ds(start, la)])
        return carry
    lax.fori_loop(0, lr, split_rhs, 0)
    loads[2].wait()

    rows_in = lax.broadcasted_iota(jnp.int32, (la, cols), 0)

    def apply_operator():
        def body(r, acc):
            at = pl.multiple_of(r * la, la)
            here = direction[pl.ds(at + la, la)]
            radial = direction[pl.ds(at, la)] + direction[pl.ds(at + 2 * la, la)]
            before = jnp.where(rows_in == 0, direction[pl.ds(left + r, 1)], pltpu.roll(here, 1, 0))
            after = jnp.where(rows_in == la - 1, direction[pl.ds(rightside + r, 1)], pltpu.roll(here, la - 1, 0))
            weight = diag[pl.ds(at, la)]
            weight = jnp.concatenate([weight] * (cols // 128), axis=1)
            got = weight * here - ((before + after) + radial)
            image[pl.ds(at, la)] = got
            store_split(at, got)
            return acc + jnp.sum((got * here).reshape(la // 8, 8, cols), axis=0)
        acc = lax.fori_loop(0, lr, body, jnp.zeros((8, cols), F32))
        return jnp.sum(acc, axis=0, keepdims=True)

    def make_lift(start, size):
        lift[pl.ds(start, size)] = basis[pl.ds(start, size)].astype(BF16)

    basis_edge = rest[-1]
    basis_copies = exchange(basis, basis_edge, basis_send, basis_recv)

    def prepare():
        row16 = lax.broadcasted_iota(jnp.int32, (kprim, 3 * kprim), 0)
        col48 = lax.broadcasted_iota(jnp.int32, (kprim, 3 * kprim), 1)
        pick_high = jnp.logical_or(col48 == row16, col48 == row16 + 2 * kprim).astype(F32).astype(BF16)
        pick_low = (col48 == row16 + kprim).astype(F32).astype(BF16)

        def turned(half, pick):
            return lax.dot_general(half, pick, (((0,), (0,)), ((), ())), preferred_element_type=F32)
        basis[pl.ds(main, ncell)] = turned(high, pick_high) + turned(low, pick_low)

        gather_edges(basis, basis_edge)
        start_exchange(basis_copies)
        make_lift(main, ncell)

        loads[3].wait()
        eye = (lax.broadcasted_iota(jnp.int32, (la, la), 0) == lax.broadcasted_iota(jnp.int32, (la, la), 1))
        for r in range(lr):
            column = jnp.sum(jnp.where(eye, cond[pl.ds(r, 1)], 0.0), axis=1, keepdims=True)
            diag[pl.ds(r * la, la)] = jnp.broadcast_to(4.0 + column, (la, 128))

    product = None
    alpha = None
    for k in range(ITERS):
        ybuf = ybufs.at[k]
        if k == 0:
            inner, coarse = apply_local(rhs, ybuf)
            curve = jnp.zeros((1, cols), F32)
        else:
            inner, coarse = apply_local(image, ybuf)
        edge = edges.at[k]
        gather_edges(ybuf, edge)
        copies = exchange(ybuf, edge, edge_send.at[k], edge_recv.at[k])
        if k == 0:
            pl.semaphore_wait(barrier, len(greeted))
        value = jnp.concatenate(
            [coarse, inner, curve, jnp.zeros((6, cols), F32)], axis=0)

        def shadow():
            start_exchange(copies)
            if k == 0:
                prepare()
        value = reduce(k, kprim + 8, value, shadow)
        coarse, inner, curve = value[:kprim], value[kprim:kprim + 1], value[kprim + 1:kprim + 2]
        if k == 0:
            loads[4].wait()
        weights, energy = lifted_weights(coarse)
        inner = inner + energy
        if k == 0:
            finish_exchange(basis_copies)
            make_lift(0, la)
            make_lift(bottom, total - bottom)
        finish_exchange(copies)
        if k == 0:
            product = inner

            def begin(i, carry):
                at = pl.multiple_of(i * step_rows, step_rows)
                got = ybuf[pl.ds(at, step_rows)] + jnp.dot(
                    lift[pl.ds(at, step_rows)], weights, preferred_element_type=F32)
                zed[pl.ds(at, step_rows)] = got
                direction[pl.ds(at, step_rows)] = got
                return carry
            lax.fori_loop(0, total // step_rows, begin, 0, unroll=True)
        else:
            alpha = product / curve
            fresh = alpha * alpha * inner - product
            ratio = fresh / product
            product = fresh

            def update(i, carry):
                at = pl.multiple_of(i * step_rows, step_rows)
                got = ybuf[pl.ds(at, step_rows)] + jnp.dot(
                    lift[pl.ds(at, step_rows)], weights, preferred_element_type=F32)
                fresh_zed = zed[pl.ds(at, step_rows)] - alpha * got
                zed[pl.ds(at, step_rows)] = fresh_zed
                old = direction[pl.ds(at, step_rows)]
                moved = alpha * old
                if k > 1:
                    moved = moved + solution_acc[pl.ds(at, step_rows)]
                solution_acc[pl.ds(at, step_rows)] = moved
                direction[pl.ds(at, step_rows)] = fresh_zed + ratio * old
                return carry
            solution_acc = rest[-2]
            lax.fori_loop(0, total // step_rows, update, 0, unroll=True)
        curve = apply_operator()
    curve = reduce(ITERS, 8, jnp.broadcast_to(curve, (8, cols)))[:1]
    alpha = product / curve

    def finish(r, carry):
        at = pl.multiple_of(r * la, la)
        out_ref[pl.ds(at, la)] = solution_acc[pl.ds(at + la, la)] + alpha * direction[pl.ds(at + la, la)]
        return carry
    lax.fori_loop(0, lr, finish, 0)
    for copy in pending:
        copy.wait_send()


def per_device(n_ang, n_rad, right_side, conduct, local_inverse, primal_basis, coarse_inverse):
    lr, la, cols = right_side.shape
    ncell, kprim = primal_basis.shape[2:]
    first, radices = stage_radices(n_ang)
    sizes = [n_rad * first] + radices
    nst = len(sizes)
    total = -(-(ncell + 2 * la + 2 * lr) // 256) * 256
    rows = kprim + 8
    dma = pltpu.SemaphoreType.DMA
    scratch = [
        pltpu.VMEM((ncell + 2 * kprim, ncell), BF16),
        pltpu.VMEM((ncell, cols), F32),
        pltpu.VMEM((ncell, 2 * cols), BF16),
        pltpu.VMEM((ncell, cols), F32),
        pltpu.VMEM((total, cols), F32),
        pltpu.VMEM((total, cols), F32),
        pltpu.VMEM((ncell, 128), F32),
        pltpu.VMEM((lr, la), F32),
        pltpu.VMEM((kprim, kprim), F32),
        pltpu.VMEM((kprim, ncell), F32),
        pltpu.VMEM((total, 3 * kprim), F32),
        pltpu.VMEM((total, 3 * kprim), BF16),
        pltpu.VMEM((ITERS, total, cols), F32),
        pltpu.VMEM((ITERS, 2, lr, cols), F32),
        pltpu.VMEM((ITERS + 1, nst, rows, cols), F32),
    ]
    scratch += [pltpu.VMEM((ITERS + 1, s - 1, rows, cols), F32) for s in sizes]
    scratch += [dma((5,)), dma((4,)), dma((4,)), dma((ITERS, 4)), dma((ITERS, 4))]
    for s in sizes:
        scratch += [dma((ITERS + 1, s - 1)), dma((ITERS + 1, s - 1))]
    scratch += [pltpu.VMEM((total, cols), F32), pltpu.VMEM((2, lr, 3 * kprim), F32)]
    flat = pl.pallas_call(
        functools.partial(kernel, (n_ang, n_rad, lr, la, cols, kprim, first, radices)),
        out_shape=jax.ShapeDtypeStruct((ncell, cols), F32),
        in_specs=[pl.BlockSpec(memory_space=pltpu.HBM)] * 5,
        out_specs=pl.BlockSpec(memory_space=pltpu.VMEM),
        scratch_shapes=scratch,
        compiler_params=pltpu.CompilerParams(
            collective_id=0, has_side_effects=True, vmem_limit_bytes=61 * 1024 * 1024),
        cost_estimate=pl.CostEstimate(
            flops=2 * ITERS * ncell * ncell * 2 * cols, bytes_accessed=5 * 1024 * 1024, transcendentals=0),
    )(right_side.reshape(ncell, cols), conduct, local_inverse.reshape(ncell, ncell),
      primal_basis.reshape(ncell, kprim).T, coarse_inverse)
    return flat.reshape(lr, la, cols)


def solution(mesh):
    return jax.shard_map(
        functools.partial(per_device, mesh.shape["ang"], mesh.shape["rad"]),
        mesh=mesh,
        in_specs=(
            P("rad", "ang", None),
            P("rad", "ang"),
            P("ang", "rad", None, None),
            P("ang", "rad", None, None),
            P(),
        ),
        out_specs=P("rad", "ang", None),
        check_vma=False,
    )
```

```python
import functools
import jax
import jax.numpy as jnp
from jax import lax
from jax.experimental import pallas as pl
from jax.experimental.pallas import tpu as pltpu
from jax.sharding import PartitionSpec as P

ITERS = 3
F32 = jnp.float32
BF16 = jnp.bfloat16
MESH = pl.DeviceIdType.MESH


def stage_radices(n_ang):
    first = 2 if n_ang % 2 == 0 else 1
    radices, rest = [], n_ang // first
    while rest > 1:
        factor = 4 if rest % 4 == 0 else next(f for f in range(2, rest + 1) if rest % f == 0)
        radices.append(factor)
        rest //= factor
    return first, radices


def split(value):
    high = value.astype(BF16)
    return high, (value - high.astype(F32)).astype(BF16)


def kernel(dims, rhs_hbm, cond_hbm, inv_hbm, basis_hbm, coarse_hbm, out_ref,
           lx, rhs, right, image, zed, direction, diag, cond, coarse_inv,
           basis_t, basis, lift, ybufs, edges, pack, *rest):
    n_ang, n_rad, lr, la, cols, kprim, first, radices = dims
    nst = 1 + len(radices)
    recvs = rest[:nst]
    (load_sem, basis_send, basis_recv, edge_send, edge_recv) = rest[nst:nst + 5]
    ar_sems = rest[nst + 5:]
    ncell = lr * la
    main, bottom = la, la + ncell
    left, rightside = bottom + la, bottom + la + lr
    total = zed.shape[0]
    step_rows = total // (total // 256)

    ang, rad = lax.axis_index("ang"), lax.axis_index("rad")
    ang_up, ang_down = lax.rem(ang + 1, n_ang), lax.rem(ang + n_ang - 1, n_ang)

    loads = [
        pltpu.make_async_copy(basis_hbm, basis_t, load_sem.at[0]),
        pltpu.make_async_copy(rhs_hbm, rhs, load_sem.at[1]),
        pltpu.make_async_copy(inv_hbm, lx.at[pl.ds(0, ncell)], load_sem.at[2]),
        pltpu.make_async_copy(cond_hbm, cond, load_sem.at[3]),
        pltpu.make_async_copy(coarse_hbm, coarse_inv, load_sem.at[4]),
    ]
    for load in loads:
        load.start()

    def partners(stage):
        found = []
        if stage == 0:
            size = n_rad * first
            low = lax.rem(ang, first)
            rank = rad * first + low
            for o in range(1, size):
                other = lax.rem(rank + o, size)
                found.append((ang - low + lax.rem(other, first), other // first))
        else:
            stride = first
            for f in radices[:stage - 1]:
                stride *= f
            f = radices[stage - 1]
            digit = lax.rem(ang // stride, f)
            for o in range(1, f):
                other = lax.rem(digit + o, f)
                found.append((ang + (other - digit) * stride, rad))
        return found

    basis[pl.ds(0, la)] = jnp.zeros((la, 128), F32)
    basis[pl.ds(bottom, total - bottom)] = jnp.zeros((total - bottom, 128), F32)
    for k in range(ITERS):
        ybufs[k, pl.ds(0, la)] = jnp.zeros((la, cols), F32)
        ybufs[k, pl.ds(bottom, total - bottom)] = jnp.zeros((total - bottom, cols), F32)

    groups = [partners(s) for s in range(nst)]
    barrier = pltpu.get_barrier_semaphore()
    greeted = [p for g in groups for p in g] + [(ang_up, rad), (ang_down, rad)]
    for peer in greeted:
        pl.semaphore_signal(barrier, inc=1, device_id=peer, device_id_type=MESH)

    def gather_edges(src, dst):
        for r in range(lr):
            dst[0, pl.ds(r, 1)] = src[pl.ds(main + r * la, 1)]
            dst[1, pl.ds(r, 1)] = src[pl.ds(main + r * la + la - 1, 1)]

    def exchange(buf, edge, send, recv):
        def remote(src, dst, i, peer):
            return pltpu.make_async_remote_copy(
                src_ref=src, dst_ref=dst, send_sem=send.at[i], recv_sem=recv.at[i],
                device_id=peer, device_id_type=MESH)
        upward = remote(buf.at[pl.ds(bottom - la, la)], buf.at[pl.ds(0, la)], 0, (ang, rad + 1))
        downward = remote(buf.at[pl.ds(main, la)], buf.at[pl.ds(bottom, la)], 1, (ang, rad - 1))
        ahead = remote(edge.at[1], buf.at[pl.ds(left, lr)], 2, (ang_up, rad))
        behind = remote(edge.at[0], buf.at[pl.ds(rightside, lr)], 3, (ang_down, rad))
        return upward, downward, ahead, behind

    def start_exchange(copies):
        upward, downward, ahead, behind = copies
        pl.when(rad < n_rad - 1)(upward.start)
        pl.when(rad > 0)(downward.start)
        ahead.start()
        behind.start()

    def finish_exchange(copies):
        upward, downward, ahead, behind = copies
        pl.when(rad > 0)(upward.wait_recv)
        pl.when(rad < n_rad - 1)(downward.wait_recv)
        ahead.wait_recv()
        behind.wait_recv()
        pl.when(rad < n_rad - 1)(upward.wait_send)
        pl.when(rad > 0)(downward.wait_send)
        ahead.wait_send()
        behind.wait_send()

    def reduce(phase, rows, value, shadow=None):
        pack[phase, 0, pl.ds(0, rows)] = value
        for stage in range(nst):
            send, recv = ar_sems[2 * stage], ar_sems[2 * stage + 1]
            copies = []
            for o, peer in enumerate(groups[stage]):
                copies.append(pltpu.make_async_remote_copy(
                    src_ref=pack.at[phase, stage, pl.ds(0, rows)],
                    dst_ref=recvs[stage].at[phase, o, pl.ds(0, rows)],
                    send_sem=send.at[phase, o], recv_sem=recv.at[phase, o],
                    device_id=peer, device_id_type=MESH))
            for copy in copies:
                copy.start()
            if stage == 0 and shadow is not None:
                shadow()
            acc = value
            for o, copy in enumerate(copies):
                copy.wait_recv()
                acc = acc + recvs[stage][phase, o, pl.ds(0, rows)]
            value = acc
            if stage + 1 < nst:
                pack[phase, stage + 1, pl.ds(0, rows)] = value
            pending.extend(copies)
        return value

    pending = []
    groups_of = cols // 128

    def fold(*values):
        pieces = [v[:, g * 128:(g + 1) * 128] for v in values for g in range(groups_of)]
        spare = -sum(p.shape[0] for p in pieces) % 8
        if spare:
            pieces.append(jnp.zeros((spare, 128), F32))
        return jnp.concatenate(pieces, axis=0)

    def unfold(value, *counts):
        found, at = [], 0
        for count in counts:
            found.append(jnp.concatenate(
                [value[at + g * count:at + (g + 1) * count] for g in range(groups_of)], axis=1))
            at += groups_of * count
        return found

    loads[0].wait()
    high, low = split(basis_t[...])
    lx[pl.ds(ncell, 2 * kprim)] = jnp.concatenate([high, low], axis=0)

    def store_split(start, value):
        high, low = split(value)
        right[pl.ds(start, la), pl.ds(0, cols)] = high
        right[pl.ds(start, la), pl.ds(cols, cols)] = low

    tile = 256 if ncell % 256 == 0 else la

    def apply_local(vec, out):
        def body(i, acc):
            start = pl.multiple_of(i * tile, tile)
            prod = jnp.dot(lx[pl.ds(start, tile)], right[...], preferred_element_type=F32)
            got = prod[:, :cols] + prod[:, cols:]
            out[pl.ds(main + start, tile)] = got
            part = got * vec[pl.ds(start, tile)]
            return acc + jnp.sum(part.reshape(tile // 8, 8, cols), axis=0)
        acc = lax.fori_loop(0, ncell // tile, body, jnp.zeros((8, cols), F32))
        small = jnp.dot(lx[pl.ds(ncell, 2 * kprim)], right[...], preferred_element_type=F32)
        both = small[:, :cols] + small[:, cols:]
        return jnp.sum(acc, axis=0, keepdims=True), both[:kprim] + both[kprim:]

    def lifted_weights(coarse):
        weights = jnp.dot(coarse_inv[...], coarse, precision=lax.Precision.HIGHEST, preferred_element_type=F32)
        high, low = split(weights)
        energy = jnp.sum(coarse * weights, axis=0, keepdims=True)
        return jnp.concatenate([high, high, low], axis=0), energy

    loads[1].wait()

    def split_rhs(r, carry):
        start = pl.multiple_of(r * la, la)
        store_split(start, rhs[pl.ds(start, la)])
        return carry
    lax.fori_loop(0, lr, split_rhs, 0)
    loads[2].wait()

    rows_in = lax.broadcasted_iota(jnp.int32, (la, cols), 0)

    def apply_operator():
        def body(r, acc):
            at = pl.multiple_of(r * la, la)
            here = direction[pl.ds(at + la, la)]
            radial = direction[pl.ds(at, la)] + direction[pl.ds(at + 2 * la, la)]
            before = jnp.where(rows_in == 0, direction[pl.ds(left + r, 1)], pltpu.roll(here, 1, 0))
            after = jnp.where(rows_in == la - 1, direction[pl.ds(rightside + r, 1)], pltpu.roll(here, la - 1, 0))
            weight = diag[pl.ds(at, la)]
            weight = jnp.concatenate([weight] * (cols // 128), axis=1)
            got = weight * here - ((before + after) + radial)
            image[pl.ds(at, la)] = got
            store_split(at, got)
            return acc + jnp.sum((got * here).reshape(la // 8, 8, cols), axis=0)
        acc = lax.fori_loop(0, lr, body, jnp.zeros((8, cols), F32))
        return jnp.sum(acc, axis=0, keepdims=True)

    def make_lift(start, size):
        lift[pl.ds(start, size)] = basis[pl.ds(start, size), pl.ds(0, 3 * kprim)].astype(BF16)

    basis_edge = rest[-1]
    basis_copies = exchange(basis, basis_edge, basis_send, basis_recv)

    def prepare():
        row16 = lax.broadcasted_iota(jnp.int32, (kprim, 128), 0)
        col48 = lax.broadcasted_iota(jnp.int32, (kprim, 128), 1)
        pick_high = jnp.logical_or(col48 == row16, col48 == row16 + 2 * kprim).astype(F32).astype(BF16)
        pick_low = (col48 == row16 + kprim).astype(F32).astype(BF16)

        def turned(half, pick):
            return lax.dot_general(half, pick, (((0,), (0,)), ((), ())), preferred_element_type=F32)
        basis[pl.ds(main, ncell)] = turned(high, pick_high) + turned(low, pick_low)

        gather_edges(basis, basis_edge)
        start_exchange(basis_copies)
        make_lift(main, ncell)

        loads[3].wait()
        eye = (lax.broadcasted_iota(jnp.int32, (la, la), 0) == lax.broadcasted_iota(jnp.int32, (la, la), 1))
        for r in range(lr):
            column = jnp.sum(jnp.where(eye, cond[pl.ds(r, 1)], 0.0), axis=1, keepdims=True)
            diag[pl.ds(r * la, la)] = jnp.broadcast_to(4.0 + column, (la, 128))

    product = None
    alpha = None
    for k in range(ITERS):
        ybuf = ybufs.at[k]
        if k == 0:
            inner, coarse = apply_local(rhs, ybuf)
            curve = jnp.zeros((1, cols), F32)
        else:
            inner, coarse = apply_local(image, ybuf)
        edge = edges.at[k]
        gather_edges(ybuf, edge)
        copies = exchange(ybuf, edge, edge_send.at[k], edge_recv.at[k])
        if k == 0:
            pl.semaphore_wait(barrier, len(greeted))
        value = fold(coarse, inner, curve)

        def shadow():
            start_exchange(copies)
            if k == 0:
                prepare()
        value = reduce(k, value.shape[0], value, shadow)
        coarse, inner, curve = unfold(value, kprim, 1, 1)
        if k == 0:
            loads[4].wait()
        weights, energy = lifted_weights(coarse)
        inner = inner + energy
        if k == 0:
            finish_exchange(basis_copies)
            make_lift(0, la)
            make_lift(bottom, total - bottom)
        finish_exchange(copies)
        if k == 0:
            product = inner

            def begin(i, carry):
                at = pl.multiple_of(i * step_rows, step_rows)
                got = ybuf[pl.ds(at, step_rows)] + jnp.dot(
                    lift[pl.ds(at, step_rows)], weights, preferred_element_type=F32)
                zed[pl.ds(at, step_rows)] = got
                direction[pl.ds(at, step_rows)] = got
                return carry
            lax.fori_loop(0, total // step_rows, begin, 0, unroll=True)
        else:
            alpha = product / curve
            fresh = alpha * alpha * inner - product
            ratio = fresh / product
            product = fresh

            def update(i, carry):
                at = pl.multiple_of(i * step_rows, step_rows)
                got = ybuf[pl.ds(at, step_rows)] + jnp.dot(
                    lift[pl.ds(at, step_rows)], weights, preferred_element_type=F32)
                fresh_zed = zed[pl.ds(at, step_rows)] - alpha * got
                zed[pl.ds(at, step_rows)] = fresh_zed
                old = direction[pl.ds(at, step_rows)]
                moved = alpha * old
                if k > 1:
                    moved = moved + solution_acc[pl.ds(at, step_rows)]
                solution_acc[pl.ds(at, step_rows)] = moved
                direction[pl.ds(at, step_rows)] = fresh_zed + ratio * old
                return carry
            solution_acc = rest[-2]
            lax.fori_loop(0, total // step_rows, update, 0, unroll=True)
        curve = apply_operator()
    value = fold(curve)
    curve, = unfold(reduce(ITERS, value.shape[0], value), 1)
    alpha = product / curve

    def finish(r, carry):
        at = pl.multiple_of(r * la, la)
        out_ref[pl.ds(at, la)] = solution_acc[pl.ds(at + la, la)] + alpha * direction[pl.ds(at + la, la)]
        return carry
    lax.fori_loop(0, lr, finish, 0)
    for copy in pending:
        copy.wait_send()


def per_device(n_ang, n_rad, right_side, conduct, local_inverse, primal_basis, coarse_inverse):
    lr, la, cols = right_side.shape
    ncell, kprim = primal_basis.shape[2:]
    first, radices = stage_radices(n_ang)
    sizes = [n_rad * first] + radices
    nst = len(sizes)
    total = -(-(ncell + 2 * la + 2 * lr) // 256) * 256
    rows = -(-(kprim + 2) * (cols // 128) // 8) * 8
    dma = pltpu.SemaphoreType.DMA
    scratch = [
        pltpu.VMEM((ncell + 2 * kprim, ncell), BF16),
        pltpu.VMEM((ncell, cols), F32),
        pltpu.VMEM((ncell, 2 * cols), BF16),
        pltpu.VMEM((ncell, cols), F32),
        pltpu.VMEM((total, cols), F32),
        pltpu.VMEM((total, cols), F32),
        pltpu.VMEM((ncell, 128), F32),
        pltpu.VMEM((lr, la), F32),
        pltpu.VMEM((kprim, kprim), F32),
        pltpu.VMEM((kprim, ncell), F32),
        pltpu.VMEM((total, 128), F32),
        pltpu.VMEM((total, 3 * kprim), BF16),
        pltpu.VMEM((ITERS, total, cols), F32),
        pltpu.VMEM((ITERS, 2, lr, cols), F32),
        pltpu.VMEM((ITERS + 1, nst, rows, 128), F32),
    ]
    scratch += [pltpu.VMEM((ITERS + 1, s - 1, rows, 128), F32) for s in sizes]
    scratch += [dma((5,)), dma((4,)), dma((4,)), dma((ITERS, 4)), dma((ITERS, 4))]
    for s in sizes:
        scratch += [dma((ITERS + 1, s - 1)), dma((ITERS + 1, s - 1))]
    scratch += [pltpu.VMEM((total, cols), F32), pltpu.VMEM((2, lr, 128), F32)]
    flat = pl.pallas_call(
        functools.partial(kernel, (n_ang, n_rad, lr, la, cols, kprim, first, radices)),
        out_shape=jax.ShapeDtypeStruct((ncell, cols), F32),
        in_specs=[pl.BlockSpec(memory_space=pltpu.HBM)] * 5,
        out_specs=pl.BlockSpec(memory_space=pltpu.VMEM),
        scratch_shapes=scratch,
        compiler_params=pltpu.CompilerParams(
            collective_id=0, has_side_effects=True, vmem_limit_bytes=61 * 1024 * 1024),
        cost_estimate=pl.CostEstimate(
            flops=2 * ITERS * ncell * ncell * 2 * cols, bytes_accessed=5 * 1024 * 1024, transcendentals=0),
    )(right_side.reshape(ncell, cols), conduct, local_inverse.reshape(ncell, ncell),
      primal_basis.reshape(ncell, kprim).T, coarse_inverse)
    return flat.reshape(lr, la, cols)


def solution(mesh):
    return jax.shard_map(
        functools.partial(per_device, mesh.shape["ang"], mesh.shape["rad"]),
        mesh=mesh,
        in_specs=(
            P("rad", "ang", None),
            P("rad", "ang"),
            P("ang", "rad", None, None),
            P("ang", "rad", None, None),
            P(),
        ),
        out_specs=P("rad", "ang", None),
        check_vma=False,
    )
```

```python
import functools
import jax
import jax.numpy as jnp
from jax import lax
from jax.experimental import pallas as pl
from jax.experimental.pallas import tpu as pltpu
from jax.sharding import PartitionSpec as P

ITERS = 3
F32 = jnp.float32
BF16 = jnp.bfloat16
MESH = pl.DeviceIdType.MESH


def stage_radices(n_ang):
    first = 2 if n_ang % 2 == 0 else 1
    radices, rest = [], n_ang // first
    while rest > 1:
        factor = 4 if rest % 4 == 0 else next(f for f in range(2, rest + 1) if rest % f == 0)
        radices.append(factor)
        rest //= factor
    return first, radices


def split(value):
    high = value.astype(BF16)
    return high, (value - high.astype(F32)).astype(BF16)


def kernel(dims, rhs_hbm, cond_hbm, inv_hbm, basis_hbm, coarse_hbm, out_ref,
           lx, rhs, right, image, zed, direction, diag, cond, coarse_inv,
           basis_t, basis, lift, ybufs, edges, pack, *rest):
    n_ang, n_rad, lr, la, cols, kprim, first, radices = dims
    nst = 1 + len(radices)
    recvs = rest[:nst]
    (load_sem, basis_send, basis_recv, edge_send, edge_recv) = rest[nst:nst + 5]
    ar_sems = rest[nst + 5:]
    ncell = lr * la
    main, bottom = la, la + ncell
    left, rightside = bottom + la, bottom + la + lr
    total = zed.shape[0]
    step_rows = total // (total // 256)

    ang, rad = lax.axis_index("ang"), lax.axis_index("rad")
    ang_up, ang_down = lax.rem(ang + 1, n_ang), lax.rem(ang + n_ang - 1, n_ang)

    loads = [
        pltpu.make_async_copy(basis_hbm, basis_t, load_sem.at[0]),
        pltpu.make_async_copy(rhs_hbm, rhs, load_sem.at[1]),
        pltpu.make_async_copy(inv_hbm, lx.at[pl.ds(0, ncell)], load_sem.at[2]),
        pltpu.make_async_copy(cond_hbm, cond, load_sem.at[3]),
        pltpu.make_async_copy(coarse_hbm, coarse_inv, load_sem.at[4]),
    ]
    for load in loads:
        load.start()

    def partners(stage):
        found = []
        if stage == 0:
            size = n_rad * first
            low = lax.rem(ang, first)
            rank = rad * first + low
            for o in range(1, size):
                other = lax.rem(rank + o, size)
                found.append((ang - low + lax.rem(other, first), other // first))
        else:
            stride = first
            for f in radices[:stage - 1]:
                stride *= f
            f = radices[stage - 1]
            digit = lax.rem(ang // stride, f)
            for o in range(1, f):
                other = lax.rem(digit + o, f)
                found.append((ang + (other - digit) * stride, rad))
        return found

    basis[pl.ds(0, la)] = jnp.zeros((la, 128), F32)
    basis[pl.ds(bottom, total - bottom)] = jnp.zeros((total - bottom, 128), F32)
    for k in range(ITERS):
        ybufs[k, pl.ds(0, la)] = jnp.zeros((la, cols), F32)
        ybufs[k, pl.ds(bottom, total - bottom)] = jnp.zeros((total - bottom, cols), F32)

    groups = [partners(s) for s in range(nst)]
    barrier = pltpu.get_barrier_semaphore()
    greeted = [p for g in groups for p in g] + [(ang_up, rad), (ang_down, rad)]
    for peer in greeted:
        pl.semaphore_signal(barrier, inc=1, device_id=peer, device_id_type=MESH)

    def gather_edges(src, dst):
        for r in range(lr):
            dst[0, pl.ds(r, 1)] = src[pl.ds(main + r * la, 1)]
            dst[1, pl.ds(r, 1)] = src[pl.ds(main + r * la + la - 1, 1)]

    def exchange(buf, edge, send, recv):
        def remote(src, dst, i, peer):
            return pltpu.make_async_remote_copy(
                src_ref=src, dst_ref=dst, send_sem=send.at[i], recv_sem=recv.at[i],
                device_id=peer, device_id_type=MESH)
        upward = remote(buf.at[pl.ds(bottom - la, la)], buf.at[pl.ds(0, la)], 0, (ang, rad + 1))
        downward = remote(buf.at[pl.ds(main, la)], buf.at[pl.ds(bottom, la)], 1, (ang, rad - 1))
        ahead = remote(edge.at[1], buf.at[pl.ds(left, lr)], 2, (ang_up, rad))
        behind = remote(edge.at[0], buf.at[pl.ds(rightside, lr)], 3, (ang_down, rad))
        return upward, downward, ahead, behind

    def start_exchange(copies):
        upward, downward, ahead, behind = copies
        pl.when(rad < n_rad - 1)(upward.start)
        pl.when(rad > 0)(downward.start)
        ahead.start()
        behind.start()

    def finish_exchange(copies):
        upward, downward, ahead, behind = copies
        pl.when(rad > 0)(upward.wait_recv)
        pl.when(rad < n_rad - 1)(downward.wait_recv)
        ahead.wait_recv()
        behind.wait_recv()
        pl.when(rad < n_rad - 1)(upward.wait_send)
        pl.when(rad > 0)(downward.wait_send)
        ahead.wait_send()
        behind.wait_send()

    def reduce(phase, rows, value, shadow=None):
        pack[phase, 0, pl.ds(0, rows)] = value
        for stage in range(nst):
            send, recv = ar_sems[2 * stage], ar_sems[2 * stage + 1]
            copies = []
            for o, peer in enumerate(groups[stage]):
                copies.append(pltpu.make_async_remote_copy(
                    src_ref=pack.at[phase, stage, pl.ds(0, rows)],
                    dst_ref=recvs[stage].at[phase, o, pl.ds(0, rows)],
                    send_sem=send.at[phase, o], recv_sem=recv.at[phase, o],
                    device_id=peer, device_id_type=MESH))
            for copy in copies:
                copy.start()
            if stage == 0 and shadow is not None:
                shadow()
            acc = value
            for o, copy in enumerate(copies):
                copy.wait_recv()
                acc = acc + recvs[stage][phase, o, pl.ds(0, rows)]
            value = acc
            if stage + 1 < nst:
                pack[phase, stage + 1, pl.ds(0, rows)] = value
            pending.extend(copies)
        return value

    pending = []
    groups_of = cols // 128

    def fold(*values):
        pieces = [v[:, g * 128:(g + 1) * 128] for v in values for g in range(groups_of)]
        spare = -sum(p.shape[0] for p in pieces) % 8
        if spare:
            pieces.append(jnp.zeros((spare, 128), F32))
        return jnp.concatenate(pieces, axis=0)

    def unfold(value, *counts):
        found, at = [], 0
        for count in counts:
            found.append(jnp.concatenate(
                [value[at + g * count:at + (g + 1) * count] for g in range(groups_of)], axis=1))
            at += groups_of * count
        return found

    loads[0].wait()
    high, low = split(basis_t[...])
    lx[pl.ds(ncell, 2 * kprim)] = jnp.concatenate([high, low], axis=0)

    def store_split(start, value):
        high, low = split(value)
        right[pl.ds(start, la), pl.ds(0, cols)] = high
        right[pl.ds(start, la), pl.ds(cols, cols)] = low

    tile = 256 if ncell % 256 == 0 else la

    def apply_local(vec, out):
        def body(i, acc):
            start = pl.multiple_of(i * tile, tile)
            prod = jnp.dot(lx[pl.ds(start, tile)], right[...], preferred_element_type=F32)
            got = prod[:, :cols] + prod[:, cols:]
            out[pl.ds(main + start, tile)] = got
            part = got * vec[pl.ds(start, tile)]
            return acc + jnp.sum(part.reshape(tile // 8, 8, cols), axis=0)
        acc = lax.fori_loop(0, ncell // tile, body, jnp.zeros((8, cols), F32))
        small = jnp.dot(lx[pl.ds(ncell, 2 * kprim)], right[...], preferred_element_type=F32)
        both = small[:, :cols] + small[:, cols:]
        return jnp.sum(acc, axis=0, keepdims=True), both[:kprim] + both[kprim:]

    def lifted_weights(coarse):
        weights = jnp.dot(coarse_inv[...], coarse, precision=lax.Precision.HIGHEST, preferred_element_type=F32)
        high, low = split(weights)
        energy = jnp.sum(coarse * weights, axis=0, keepdims=True)
        return jnp.concatenate([high, high, low], axis=0), energy

    loads[1].wait()

    def split_rhs(r, carry):
        start = pl.multiple_of(r * la, la)
        store_split(start, rhs[pl.ds(start, la)])
        return carry
    lax.fori_loop(0, lr, split_rhs, 0)
    loads[2].wait()

    rows_in = lax.broadcasted_iota(jnp.int32, (la, cols), 0)

    def apply_operator():
        def body(r, acc):
            at = pl.multiple_of(r * la, la)
            here = direction[pl.ds(at + la, la)]
            radial = direction[pl.ds(at, la)] + direction[pl.ds(at + 2 * la, la)]
            before = jnp.where(rows_in == 0, direction[pl.ds(left + r, 1)], pltpu.roll(here, 1, 0))
            after = jnp.where(rows_in == la - 1, direction[pl.ds(rightside + r, 1)], pltpu.roll(here, la - 1, 0))
            weight = diag[pl.ds(at, la)]
            weight = jnp.concatenate([weight] * (cols // 128), axis=1)
            got = weight * here - ((before + after) + radial)
            image[pl.ds(at, la)] = got
            store_split(at, got)
            return acc + jnp.sum((got * here).reshape(la // 8, 8, cols), axis=0)
        acc = lax.fori_loop(0, lr, body, jnp.zeros((8, cols), F32))
        return jnp.sum(acc, axis=0, keepdims=True)

    def make_lift(start, size):
        lift[pl.ds(start, size)] = basis[pl.ds(start, size), pl.ds(0, 3 * kprim)].astype(BF16)

    basis_edge = rest[-1]
    basis_copies = exchange(basis, basis_edge, basis_send, basis_recv)

    def send_basis():
        row16 = lax.broadcasted_iota(jnp.int32, (kprim, 128), 0)
        col48 = lax.broadcasted_iota(jnp.int32, (kprim, 128), 1)
        pick_high = jnp.logical_or(col48 == row16, col48 == row16 + 2 * kprim).astype(F32).astype(BF16)
        pick_low = (col48 == row16 + kprim).astype(F32).astype(BF16)

        def turned(half, pick):
            return lax.dot_general(half, pick, (((0,), (0,)), ((), ())), preferred_element_type=F32)
        basis[pl.ds(main, ncell)] = turned(high, pick_high) + turned(low, pick_low)

        gather_edges(basis, basis_edge)
        start_exchange(basis_copies)

    def prepare():
        make_lift(main, ncell)
        loads[3].wait()
        eye = (lax.broadcasted_iota(jnp.int32, (la, la), 0) == lax.broadcasted_iota(jnp.int32, (la, la), 1))
        for r in range(lr):
            column = jnp.sum(jnp.where(eye, cond[pl.ds(r, 1)], 0.0), axis=1, keepdims=True)
            diag[pl.ds(r * la, la)] = jnp.broadcast_to(4.0 + column, (la, 128))

    product = None
    alpha = None
    for k in range(ITERS):
        ybuf = ybufs.at[k]
        if k == 0:
            pl.semaphore_wait(barrier, len(greeted))
            send_basis()
            inner, coarse = apply_local(rhs, ybuf)
            curve = jnp.zeros((1, cols), F32)
        else:
            inner, coarse = apply_local(image, ybuf)
        edge = edges.at[k]
        gather_edges(ybuf, edge)
        copies = exchange(ybuf, edge, edge_send.at[k], edge_recv.at[k])
        value = fold(coarse, inner, curve)

        def shadow():
            start_exchange(copies)
            if k == 0:
                prepare()
        value = reduce(k, value.shape[0], value, shadow)
        coarse, inner, curve = unfold(value, kprim, 1, 1)
        if k == 0:
            loads[4].wait()
        weights, energy = lifted_weights(coarse)
        inner = inner + energy
        if k == 0:
            finish_exchange(basis_copies)
            make_lift(0, la)
            make_lift(bottom, total - bottom)
        finish_exchange(copies)
        if k == 0:
            product = inner

            def begin(i, carry):
                at = pl.multiple_of(i * step_rows, step_rows)
                got = ybuf[pl.ds(at, step_rows)] + jnp.dot(
                    lift[pl.ds(at, step_rows)], weights, preferred_element_type=F32)
                zed[pl.ds(at, step_rows)] = got
                direction[pl.ds(at, step_rows)] = got
                return carry
            lax.fori_loop(0, total // step_rows, begin, 0, unroll=True)
        else:
            alpha = product / curve
            fresh = alpha * alpha * inner - product
            ratio = fresh / product
            product = fresh

            def update(i, carry):
                at = pl.multiple_of(i * step_rows, step_rows)
                got = ybuf[pl.ds(at, step_rows)] + jnp.dot(
                    lift[pl.ds(at, step_rows)], weights, preferred_element_type=F32)
                fresh_zed = zed[pl.ds(at, step_rows)] - alpha * got
                zed[pl.ds(at, step_rows)] = fresh_zed
                old = direction[pl.ds(at, step_rows)]
                moved = alpha * old
                if k > 1:
                    moved = moved + solution_acc[pl.ds(at, step_rows)]
                solution_acc[pl.ds(at, step_rows)] = moved
                direction[pl.ds(at, step_rows)] = fresh_zed + ratio * old
                return carry
            solution_acc = rest[-2]
            lax.fori_loop(0, total // step_rows, update, 0, unroll=True)
        curve = apply_operator()
    value = fold(curve)
    curve, = unfold(reduce(ITERS, value.shape[0], value), 1)
    alpha = product / curve

    part = ncell // 4
    stores = []
    for i in range(4):
        at = i * part
        solution_acc[pl.ds(at + la, part)] = (
            solution_acc[pl.ds(at + la, part)] + alpha * direction[pl.ds(at + la, part)])
        stores.append(pltpu.make_async_copy(
            solution_acc.at[pl.ds(at + la, part)], out_ref.at[pl.ds(at, part)], load_sem.at[5 + i]))
        stores[-1].start()
    for store in stores:
        store.wait()
    for copy in pending:
        copy.wait_send()


def per_device(n_ang, n_rad, right_side, conduct, local_inverse, primal_basis, coarse_inverse):
    lr, la, cols = right_side.shape
    ncell, kprim = primal_basis.shape[2:]
    first, radices = stage_radices(n_ang)
    sizes = [n_rad * first] + radices
    nst = len(sizes)
    total = -(-(ncell + 2 * la + 2 * lr) // 256) * 256
    rows = -(-(kprim + 2) * (cols // 128) // 8) * 8
    dma = pltpu.SemaphoreType.DMA
    scratch = [
        pltpu.VMEM((ncell + 2 * kprim, ncell), BF16),
        pltpu.VMEM((ncell, cols), F32),
        pltpu.VMEM((ncell, 2 * cols), BF16),
        pltpu.VMEM((ncell, cols), F32),
        pltpu.VMEM((total, cols), F32),
        pltpu.VMEM((total, cols), F32),
        pltpu.VMEM((ncell, 128), F32),
        pltpu.VMEM((lr, la), F32),
        pltpu.VMEM((kprim, kprim), F32),
        pltpu.VMEM((kprim, ncell), F32),
        pltpu.VMEM((total, 128), F32),
        pltpu.VMEM((total, 3 * kprim), BF16),
        pltpu.VMEM((ITERS, total, cols), F32),
        pltpu.VMEM((ITERS, 2, lr, cols), F32),
        pltpu.VMEM((ITERS + 1, nst, rows, 128), F32),
    ]
    scratch += [pltpu.VMEM((ITERS + 1, s - 1, rows, 128), F32) for s in sizes]
    scratch += [dma((9,)), dma((4,)), dma((4,)), dma((ITERS, 4)), dma((ITERS, 4))]
    for s in sizes:
        scratch += [dma((ITERS + 1, s - 1)), dma((ITERS + 1, s - 1))]
    scratch += [pltpu.VMEM((total, cols), F32), pltpu.VMEM((2, lr, 128), F32)]
    flat = pl.pallas_call(
        functools.partial(kernel, (n_ang, n_rad, lr, la, cols, kprim, first, radices)),
        out_shape=jax.ShapeDtypeStruct((ncell, cols), F32),
        in_specs=[pl.BlockSpec(memory_space=pltpu.HBM)] * 5,
        out_specs=pl.BlockSpec(memory_space=pltpu.HBM),
        scratch_shapes=scratch,
        compiler_params=pltpu.CompilerParams(
            collective_id=0, has_side_effects=True, vmem_limit_bytes=61 * 1024 * 1024),
        cost_estimate=pl.CostEstimate(
            flops=2 * ITERS * ncell * ncell * 2 * cols, bytes_accessed=5 * 1024 * 1024, transcendentals=0),
    )(right_side.reshape(ncell, cols), conduct, local_inverse.reshape(ncell, ncell),
      primal_basis.reshape(ncell, kprim).T, coarse_inverse)
    return flat.reshape(lr, la, cols)


def solution(mesh):
    return jax.shard_map(
        functools.partial(per_device, mesh.shape["ang"], mesh.shape["rad"]),
        mesh=mesh,
        in_specs=(
            P("rad", "ang", None),
            P("rad", "ang"),
            P("ang", "rad", None, None),
            P("ang", "rad", None, None),
            P(),
        ),
        out_specs=P("rad", "ang", None),
        check_vma=False,
    )
```

```python
import functools
import jax
import jax.numpy as jnp
from jax import lax
from jax.experimental import pallas as pl
from jax.experimental.pallas import tpu as pltpu
from jax.sharding import PartitionSpec as P

ITERS = 3
F32 = jnp.float32
BF16 = jnp.bfloat16
MESH = pl.DeviceIdType.MESH


def stage_radices(n_ang):
    first = 2 if n_ang % 2 == 0 else 1
    radices, rest = [], n_ang // first
    while rest > 1:
        factor = 4 if rest % 4 == 0 else next(f for f in range(2, rest + 1) if rest % f == 0)
        radices.append(factor)
        rest //= factor
    return first, radices


def split(value):
    high = value.astype(BF16)
    return high, (value - high.astype(F32)).astype(BF16)


def kernel(dims, rhs_hbm, cond_hbm, inv_hbm, basis_hbm, coarse_hbm, out_ref,
           lx, rhs, right, image, zed, direction, diag, cond, coarse_inv,
           basis_t, basis, lift, ybufs, edges, pack, *rest):
    n_ang, n_rad, lr, la, cols, kprim, first, radices = dims
    nst = 1 + len(radices)
    recvs = rest[:nst]
    (load_sem, basis_send, basis_recv, edge_send, edge_recv) = rest[nst:nst + 5]
    ar_sems = rest[nst + 5:]
    ncell = lr * la
    main, bottom = la, la + ncell
    left, rightside = bottom + la, bottom + la + lr
    total = zed.shape[0]
    step_rows = total // (total // 256)

    ang, rad = lax.axis_index("ang"), lax.axis_index("rad")
    ang_up, ang_down = lax.rem(ang + 1, n_ang), lax.rem(ang + n_ang - 1, n_ang)

    loads = [
        pltpu.make_async_copy(basis_hbm, basis_t, load_sem.at[0]),
        pltpu.make_async_copy(rhs_hbm, rhs, load_sem.at[1]),
        pltpu.make_async_copy(inv_hbm, lx.at[pl.ds(0, ncell)], load_sem.at[2]),
        pltpu.make_async_copy(cond_hbm, cond, load_sem.at[3]),
        pltpu.make_async_copy(coarse_hbm, coarse_inv, load_sem.at[4]),
    ]
    for load in loads:
        load.start()

    def partners(stage):
        found = []
        if stage == 0:
            size = n_rad * first
            low = lax.rem(ang, first)
            rank = rad * first + low
            for o in range(1, size):
                other = lax.rem(rank + o, size)
                found.append((ang - low + lax.rem(other, first), other // first))
        else:
            stride = first
            for f in radices[:stage - 1]:
                stride *= f
            f = radices[stage - 1]
            digit = lax.rem(ang // stride, f)
            for o in range(1, f):
                other = lax.rem(digit + o, f)
                found.append((ang + (other - digit) * stride, rad))
        return found

    basis[pl.ds(0, la)] = jnp.zeros((la, 128), F32)
    basis[pl.ds(bottom, total - bottom)] = jnp.zeros((total - bottom, 128), F32)
    for k in range(ITERS):
        ybufs[k, pl.ds(0, la)] = jnp.zeros((la, cols), F32)
        ybufs[k, pl.ds(bottom, total - bottom)] = jnp.zeros((total - bottom, cols), F32)

    groups = [partners(s) for s in range(nst)]
    barrier = pltpu.get_barrier_semaphore()
    greeted = [p for g in groups for p in g] + [(ang_up, rad), (ang_down, rad)]
    for peer in greeted:
        pl.semaphore_signal(barrier, inc=1, device_id=peer, device_id_type=MESH)

    def gather_edges(src, dst):
        for r in range(lr):
            dst[0, pl.ds(r, 1)] = src[pl.ds(main + r * la, 1)]
            dst[1, pl.ds(r, 1)] = src[pl.ds(main + r * la + la - 1, 1)]

    def exchange(buf, edge, send, recv):
        def remote(src, dst, i, peer):
            return pltpu.make_async_remote_copy(
                src_ref=src, dst_ref=dst, send_sem=send.at[i], recv_sem=recv.at[i],
                device_id=peer, device_id_type=MESH)
        upward = remote(buf.at[pl.ds(bottom - la, la)], buf.at[pl.ds(0, la)], 0, (ang, rad + 1))
        downward = remote(buf.at[pl.ds(main, la)], buf.at[pl.ds(bottom, la)], 1, (ang, rad - 1))
        ahead = remote(edge.at[1], buf.at[pl.ds(left, lr)], 2, (ang_up, rad))
        behind = remote(edge.at[0], buf.at[pl.ds(rightside, lr)], 3, (ang_down, rad))
        return upward, downward, ahead, behind

    def start_exchange(copies):
        upward, downward, ahead, behind = copies
        pl.when(rad < n_rad - 1)(upward.start)
        pl.when(rad > 0)(downward.start)
        ahead.start()
        behind.start()

    def finish_exchange(copies):
        upward, downward, ahead, behind = copies
        pl.when(rad > 0)(upward.wait_recv)
        pl.when(rad < n_rad - 1)(downward.wait_recv)
        ahead.wait_recv()
        behind.wait_recv()
        pl.when(rad < n_rad - 1)(upward.wait_send)
        pl.when(rad > 0)(downward.wait_send)
        ahead.wait_send()
        behind.wait_send()

    def reduce(phase, rows, value, shadow=None):
        pack[phase, 0, pl.ds(0, rows)] = value
        for stage in range(nst):
            send, recv = ar_sems[2 * stage], ar_sems[2 * stage + 1]
            copies = []
            for o, peer in enumerate(groups[stage]):
                copies.append(pltpu.make_async_remote_copy(
                    src_ref=pack.at[phase, stage, pl.ds(0, rows)],
                    dst_ref=recvs[stage].at[phase, o, pl.ds(0, rows)],
                    send_sem=send.at[phase, o], recv_sem=recv.at[phase, o],
                    device_id=peer, device_id_type=MESH))
            for copy in copies:
                copy.start()
            if stage == 0 and shadow is not None:
                shadow()
            acc = value
            for o, copy in enumerate(copies):
                copy.wait_recv()
                acc = acc + recvs[stage][phase, o, pl.ds(0, rows)]
            value = acc
            if stage + 1 < nst:
                pack[phase, stage + 1, pl.ds(0, rows)] = value
            pending.extend(copies)
        return value

    pending = []
    groups_of = cols // 128

    def fold(*values):
        pieces = [v[:, g * 128:(g + 1) * 128] for v in values for g in range(groups_of)]
        spare = -sum(p.shape[0] for p in pieces) % 8
        if spare:
            pieces.append(jnp.zeros((spare, 128), F32))
        return jnp.concatenate(pieces, axis=0)

    def unfold(value, *counts):
        found, at = [], 0
        for count in counts:
            found.append(jnp.concatenate(
                [value[at + g * count:at + (g + 1) * count] for g in range(groups_of)], axis=1))
            at += groups_of * count
        return found

    loads[0].wait()
    high, low = split(basis_t[...])
    lx[pl.ds(ncell, 2 * kprim)] = jnp.concatenate([high, low], axis=0)

    def store_split(start, value):
        high, low = split(value)
        right[pl.ds(start, la), pl.ds(0, cols)] = high
        right[pl.ds(start, la), pl.ds(cols, cols)] = low

    tile = 256 if ncell % 256 == 0 else la

    def apply_local(vec, out):
        def body(i, acc):
            start = pl.multiple_of(i * tile, tile)
            prod = jnp.dot(lx[pl.ds(start, tile)], right[...], preferred_element_type=F32)
            got = prod[:, :cols] + prod[:, cols:]
            out[pl.ds(main + start, tile)] = got
            part = got * vec[pl.ds(start, tile)]
            return acc + jnp.sum(part.reshape(tile // 8, 8, cols), axis=0)
        acc = lax.fori_loop(0, ncell // tile, body, jnp.zeros((8, cols), F32), unroll=True)
        small = jnp.dot(lx[pl.ds(ncell, 2 * kprim)], right[...], preferred_element_type=F32)
        both = small[:, :cols] + small[:, cols:]
        return jnp.sum(acc, axis=0, keepdims=True), both[:kprim] + both[kprim:]

    def lifted_weights(coarse):
        weights = jnp.dot(coarse_inv[...], coarse, precision=lax.Precision.HIGHEST, preferred_element_type=F32)
        high, low = split(weights)
        energy = jnp.sum(coarse * weights, axis=0, keepdims=True)
        return jnp.concatenate([high, high, low], axis=0), energy

    loads[1].wait()

    def split_rhs(r, carry):
        start = pl.multiple_of(r * la, la)
        store_split(start, rhs[pl.ds(start, la)])
        return carry
    lax.fori_loop(0, lr, split_rhs, 0)
    loads[2].wait()

    rows_in = lax.broadcasted_iota(jnp.int32, (la, cols), 0)

    def apply_operator():
        def body(r, acc):
            at = pl.multiple_of(r * la, la)
            here = direction[pl.ds(at + la, la)]
            radial = direction[pl.ds(at, la)] + direction[pl.ds(at + 2 * la, la)]
            before = jnp.where(rows_in == 0, direction[pl.ds(left + r, 1)], pltpu.roll(here, 1, 0))
            after = jnp.where(rows_in == la - 1, direction[pl.ds(rightside + r, 1)], pltpu.roll(here, la - 1, 0))
            weight = diag[pl.ds(at, la)]
            weight = jnp.concatenate([weight] * (cols // 128), axis=1)
            got = weight * here - ((before + after) + radial)
            image[pl.ds(at, la)] = got
            store_split(at, got)
            return acc + jnp.sum((got * here).reshape(la // 8, 8, cols), axis=0)
        acc = lax.fori_loop(0, lr, body, jnp.zeros((8, cols), F32), unroll=4)
        return jnp.sum(acc, axis=0, keepdims=True)

    def make_lift(start, size):
        lift[pl.ds(start, size)] = basis[pl.ds(start, size), pl.ds(0, 3 * kprim)].astype(BF16)

    basis_edge = rest[-1]
    basis_copies = exchange(basis, basis_edge, basis_send, basis_recv)

    def prepare():
        row16 = lax.broadcasted_iota(jnp.int32, (kprim, 128), 0)
        col48 = lax.broadcasted_iota(jnp.int32, (kprim, 128), 1)
        pick_high = jnp.logical_or(col48 == row16, col48 == row16 + 2 * kprim).astype(F32).astype(BF16)
        pick_low = (col48 == row16 + kprim).astype(F32).astype(BF16)

        def turned(half, pick):
            return lax.dot_general(half, pick, (((0,), (0,)), ((), ())), preferred_element_type=F32)
        basis[pl.ds(main, ncell)] = turned(high, pick_high) + turned(low, pick_low)

        gather_edges(basis, basis_edge)
        start_exchange(basis_copies)
        make_lift(main, ncell)

        loads[3].wait()
        eye = (lax.broadcasted_iota(jnp.int32, (la, la), 0) == lax.broadcasted_iota(jnp.int32, (la, la), 1))
        for r in range(lr):
            column = jnp.sum(jnp.where(eye, cond[pl.ds(r, 1)], 0.0), axis=1, keepdims=True)
            diag[pl.ds(r * la, la)] = jnp.broadcast_to(4.0 + column, (la, 128))

    product = None
    alpha = None
    for k in range(ITERS):
        ybuf = ybufs.at[k]
        if k == 0:
            inner, coarse = apply_local(rhs, ybuf)
            curve = jnp.zeros((1, cols), F32)
        else:
            inner, coarse = apply_local(image, ybuf)
        edge = edges.at[k]
        gather_edges(ybuf, edge)
        copies = exchange(ybuf, edge, edge_send.at[k], edge_recv.at[k])
        if k == 0:
            pl.semaphore_wait(barrier, len(greeted))
        value = fold(coarse, inner, curve)

        def shadow():
            start_exchange(copies)
            if k == 0:
                prepare()
        value = reduce(k, value.shape[0], value, shadow)
        coarse, inner, curve = unfold(value, kprim, 1, 1)
        if k == 0:
            loads[4].wait()
        weights, energy = lifted_weights(coarse)
        inner = inner + energy
        if k == 0:
            finish_exchange(basis_copies)
            make_lift(0, la)
            make_lift(bottom, total - bottom)
        finish_exchange(copies)
        if k == 0:
            product = inner

            def begin(i, carry):
                at = pl.multiple_of(i * step_rows, step_rows)
                got = ybuf[pl.ds(at, step_rows)] + jnp.dot(
                    lift[pl.ds(at, step_rows)], weights, preferred_element_type=F32)
                zed[pl.ds(at, step_rows)] = got
                direction[pl.ds(at, step_rows)] = got
                return carry
            lax.fori_loop(0, total // step_rows, begin, 0, unroll=True)
        else:
            alpha = product / curve
            fresh = alpha * alpha * inner - product
            ratio = fresh / product
            product = fresh

            def update(i, carry):
                at = pl.multiple_of(i * step_rows, step_rows)
                got = ybuf[pl.ds(at, step_rows)] + jnp.dot(
                    lift[pl.ds(at, step_rows)], weights, preferred_element_type=F32)
                fresh_zed = zed[pl.ds(at, step_rows)] - alpha * got
                zed[pl.ds(at, step_rows)] = fresh_zed
                old = direction[pl.ds(at, step_rows)]
                moved = alpha * old
                if k > 1:
                    moved = moved + solution_acc[pl.ds(at, step_rows)]
                solution_acc[pl.ds(at, step_rows)] = moved
                direction[pl.ds(at, step_rows)] = fresh_zed + ratio * old
                return carry
            solution_acc = rest[-2]
            lax.fori_loop(0, total // step_rows, update, 0, unroll=True)
        curve = apply_operator()
    value = fold(curve)
    curve, = unfold(reduce(ITERS, value.shape[0], value), 1)
    alpha = product / curve

    def finish(r, carry):
        at = pl.multiple_of(r * la, la)
        out_ref[pl.ds(at, la)] = solution_acc[pl.ds(at + la, la)] + alpha * direction[pl.ds(at + la, la)]
        return carry
    lax.fori_loop(0, lr, finish, 0)
    for copy in pending:
        copy.wait_send()


def per_device(n_ang, n_rad, right_side, conduct, local_inverse, primal_basis, coarse_inverse):
    lr, la, cols = right_side.shape
    ncell, kprim = primal_basis.shape[2:]
    first, radices = stage_radices(n_ang)
    sizes = [n_rad * first] + radices
    nst = len(sizes)
    total = -(-(ncell + 2 * la + 2 * lr) // 256) * 256
    rows = -(-(kprim + 2) * (cols // 128) // 8) * 8
    dma = pltpu.SemaphoreType.DMA
    scratch = [
        pltpu.VMEM((ncell + 2 * kprim, ncell), BF16),
        pltpu.VMEM((ncell, cols), F32),
        pltpu.VMEM((ncell, 2 * cols), BF16),
        pltpu.VMEM((ncell, cols), F32),
        pltpu.VMEM((total, cols), F32),
        pltpu.VMEM((total, cols), F32),
        pltpu.VMEM((ncell, 128), F32),
        pltpu.VMEM((lr, la), F32),
        pltpu.VMEM((kprim, kprim), F32),
        pltpu.VMEM((kprim, ncell), F32),
        pltpu.VMEM((total, 128), F32),
        pltpu.VMEM((total, 3 * kprim), BF16),
        pltpu.VMEM((ITERS, total, cols), F32),
        pltpu.VMEM((ITERS, 2, lr, cols), F32),
        pltpu.VMEM((ITERS + 1, nst, rows, 128), F32),
    ]
    scratch += [pltpu.VMEM((ITERS + 1, s - 1, rows, 128), F32) for s in sizes]
    scratch += [dma((5,)), dma((4,)), dma((4,)), dma((ITERS, 4)), dma((ITERS, 4))]
    for s in sizes:
        scratch += [dma((ITERS + 1, s - 1)), dma((ITERS + 1, s - 1))]
    scratch += [pltpu.VMEM((total, cols), F32), pltpu.VMEM((2, lr, 128), F32)]
    flat = pl.pallas_call(
        functools.partial(kernel, (n_ang, n_rad, lr, la, cols, kprim, first, radices)),
        out_shape=jax.ShapeDtypeStruct((ncell, cols), F32),
        in_specs=[pl.BlockSpec(memory_space=pltpu.HBM)] * 5,
        out_specs=pl.BlockSpec(memory_space=pltpu.VMEM),
        scratch_shapes=scratch,
        compiler_params=pltpu.CompilerParams(
            collective_id=0, has_side_effects=True, vmem_limit_bytes=61 * 1024 * 1024),
        cost_estimate=pl.CostEstimate(
            flops=2 * ITERS * ncell * ncell * 2 * cols, bytes_accessed=5 * 1024 * 1024, transcendentals=0),
    )(right_side.reshape(ncell, cols), conduct, local_inverse.reshape(ncell, ncell),
      primal_basis.reshape(ncell, kprim).T, coarse_inverse)
    return flat.reshape(lr, la, cols)


def solution(mesh):
    return jax.shard_map(
        functools.partial(per_device, mesh.shape["ang"], mesh.shape["rad"]),
        mesh=mesh,
        in_specs=(
            P("rad", "ang", None),
            P("rad", "ang"),
            P("ang", "rad", None, None),
            P("ang", "rad", None, None),
            P(),
        ),
        out_specs=P("rad", "ang", None),
        check_vma=False,
    )
```
